256 devices in a mesh: blk: 64 (over z, y, core), rep: 4 (over x).
Axes of the slice: x: 4, y: 4, z: 8, core: 2. Of those that a mesh axis runs over, the one named last changes fastest.
Arguments:
- embeddings: bfloat16 [524288, 1024], P(('blk', 'rep'))
- destination: int32 [524288], P(('blk', 'rep')), may hold values from 0 to 524287, as said below
- arrival: int32 [524288], P(('blk', 'rep')), may hold values from 0 to 3071, as said below
- dataset_index: int32 [524288], replicated, may hold values from 0 to 524287, each once
Outputs:
- best_similarity: float32 [524288], P(('blk', 'rep'))
The draws below stay inside these ranges and needn't reach their ends.
Inputs may be any that keep to these rules, and one draw needn't show every extreme that they name: A permutation. The rows of one source block of 2048 rows go to 256 target blocks destination // 2048 (all blocks when 2 * 128 equals their number), with any index along rep; no source block sends more than 12 rows to one target block, and every source block sends exactly 12 to some. Consistent with destination: the row named by arrival[p] is the stored row whose destination is p.
All inputs are finite; a program needn't handle non-finite values.
Results may differ from the reference program's by a relative error of at most 0.00043.
Values may be sent and summed in bfloat16 or wider, within the bound.
A program may use at most 64 MiB of HBM per device.

```python
import math
import jax
import jax.numpy as jnp
from jax import lax

D = 1024
R_DEV = 2048
SPREAD = 128
CAP = 12
ROWS = 524288
CLUSTERS = 128
N_BLK = 64
N_REP = 4
DEVICES = 256


def rank_within(targets):
    onehot = (targets[:, None] == jnp.arange(DEVICES, dtype=jnp.int32)[None, :]).astype(jnp.int32)
    return jnp.sum((jnp.cumsum(onehot, axis=0) - 1) * onehot, axis=1).astype(jnp.int32)


def regroup_plan(key):
    shift_amount = jax.random.randint(jax.random.fold_in(key, 11), (), 0, DEVICES)
    unit_count = R_DEV // (4 * SPREAD)
    offsets = jnp.arange(DEVICES, dtype=jnp.int32)
    lagged = (offsets[None, :] - offsets[:, None] + shift_amount) % DEVICES
    counts = jnp.where(lagged < 2 * SPREAD, jnp.where(lagged % 2 == 0, 3 * unit_count, unit_count), 0).astype(jnp.int32)
    send_end = jnp.cumsum(counts, axis=1).astype(jnp.int32)
    recv_start = (jnp.cumsum(counts, axis=0) - counts).astype(jnp.int32)
    sorted_pos = jnp.arange(R_DEV, dtype=jnp.int32)
    target_sorted = jax.vmap(lambda ends: jnp.searchsorted(ends, sorted_pos, side='right'))(send_end).astype(jnp.int32)
    row_keys = jax.random.split(jax.random.fold_in(key, 12), DEVICES)
    slot_keys = jax.random.split(jax.random.fold_in(key, 13), DEVICES)
    row_perm = jax.vmap(lambda one_key: jax.random.permutation(one_key, R_DEV))(row_keys).astype(jnp.int32)
    slot_perm = jax.vmap(lambda one_key: jax.random.permutation(one_key, R_DEV))(slot_keys).astype(jnp.int32)
    target_rows = jnp.zeros((DEVICES, R_DEV), jnp.int32).at[offsets[:, None], row_perm].set(target_sorted)
    within = lax.map(rank_within, target_rows)
    sender = jnp.broadcast_to(offsets[:, None], (DEVICES, R_DEV))
    slot_sorted = recv_start[sender, target_rows] + within
    slot_final = slot_perm[target_rows, slot_sorted]
    destination = (target_rows * R_DEV + slot_final).reshape(ROWS).astype(jnp.int32)
    arrival = jnp.zeros((ROWS,), jnp.int32).at[destination].set((sender * CAP + within).reshape(ROWS))
    return (destination, arrival)


def draw_destination(key, part):
    destination, arrival = regroup_plan(key)
    return destination


def draw_arrival(key, part):
    destination, arrival = regroup_plan(key)
    return arrival


def draw_embeddings(key, part):
    destination, arrival = regroup_plan(key)
    key = jax.random.fold_in(key, 1)
    noise_key, sigma_key, centre_key, mix_key = jax.random.split(key, 4)
    noise = jax.random.normal(noise_key, (ROWS, D), jnp.float32)
    sigma = jnp.exp(jax.random.uniform(sigma_key, (ROWS,), jnp.float32, -0.6931472, 0.6931472))
    centres = jax.random.normal(centre_key, (CLUSTERS, D), jnp.float32)
    block_id = destination // R_DEV
    blk_position = block_id // N_REP
    cluster = blk_position // 2 * N_REP + block_id % N_REP
    in_second = (blk_position % 2).astype(jnp.float32)
    source_of_pos = jnp.zeros((ROWS,), jnp.int32).at[destination].set(jnp.arange(ROWS, dtype=jnp.int32))
    partner_pos = jnp.where(blk_position % 2 == 1, destination - N_REP * R_DEV, destination)
    partner_row = source_of_pos[partner_pos]
    mixing = jax.random.uniform(mix_key, (ROWS,), jnp.float32, 0.0, 0.95) * in_second
    shared = mixing[:, None] * noise[partner_row] + jnp.sqrt(1.0 - mixing * mixing)[:, None] * noise
    values = centres[cluster] + sigma[:, None] * shared
    return values.astype(jnp.bfloat16)


def setup_inputs(seed: int = 0) -> dict:
    keys = jax.random.split(jax.random.key(seed), 5)
    embeddings = draw_embeddings(jax.random.fold_in(keys[4], 71), 0)
    destination = draw_destination(jax.random.fold_in(keys[4], 71), 0)
    arrival = draw_arrival(jax.random.fold_in(keys[4], 71), 0)
    dataset_index = jax.random.permutation(keys[3], ROWS).astype(jnp.int32)
    return dict(embeddings=embeddings, destination=destination, arrival=arrival, dataset_index=dataset_index)


def normalize(raw_rows):
    widened = raw_rows.astype(jnp.float32)
    row_scale = lax.rsqrt(lax.optimization_barrier(jnp.mean(widened * widened, axis=1, keepdims=True)) + 1e-06) / math.sqrt(widened.shape[1])
    return (widened * row_scale).astype(jnp.bfloat16)

def count_block(targets):
    onehot = (targets[:, None] == jnp.arange(DEVICES, dtype=jnp.int32)[None, :]).astype(jnp.int32)
    return lax.optimization_barrier(jnp.sum((jnp.cumsum(onehot, axis=0) - 1) * onehot, axis=1)).astype(jnp.int32)

def cluster_best(pieces):
    raw_rows, rank_rows = pieces
    normal_rows = normalize(raw_rows)
    scores = lax.dot_general(normal_rows, normal_rows, (((1,), (1,)), ((), ())), preferred_element_type=jnp.float32)
    earlier = rank_rows[None, :] < rank_rows[:, None]
    return lax.optimization_barrier(jnp.max(jnp.where(earlier, scores, jnp.float32(-1.0)), axis=1))

def reference(embeddings, destination, arrival, dataset_index):
    source = jnp.arange(ROWS, dtype=jnp.int32)
    sender = source // R_DEV
    target = (destination // R_DEV).astype(jnp.int32)
    within = lax.map(count_block, target.reshape(DEVICES, R_DEV)).reshape(ROWS)
    slot_index = (target * DEVICES + sender) * CAP + within
    slot_table = jnp.zeros((DEVICES * DEVICES * CAP,), jnp.int32).at[slot_index].set(source)
    owner_block = source // R_DEV
    picked = slot_table[owner_block * DEVICES * CAP + arrival]
    grouped = embeddings[picked]
    half_blk = N_BLK // 2
    clustered = grouped.reshape(half_blk, 2, N_REP, R_DEV, D).transpose(0, 2, 1, 3, 4).reshape(CLUSTERS, 2 * R_DEV, D)
    cluster_ranks = dataset_index.reshape(half_blk, 2, N_REP, R_DEV).transpose(0, 2, 1, 3).reshape(CLUSTERS, 2 * R_DEV)
    best = lax.map(cluster_best, (clustered, cluster_ranks))
    return best.reshape(half_blk, N_REP, 2, R_DEV).transpose(0, 2, 1, 3).reshape(ROWS)
```

```python
import math

import jax
import jax.numpy as jnp
import numpy as np
from jax import lax
from jax.experimental import pallas as pl
from jax.experimental.pallas import tpu as pltpu
from jax.sharding import PartitionSpec as P

MESH = pl.DeviceIdType.MESH
ROWS = 2048
FEAT = 1024
CAP = 12
DEV = 256
PLANE = 32
GROUPS = 8
GS = PLANE * CAP
SLOTS = DEV * CAP
WIDE = 256
PARTS = FEAT // WIDE
MR = CAP * PARTS
QUAD = 4 * MR
GR = PLANE * MR
NOBODY = 2.0**23


def swap_matrix():
    r = np.arange(QUAD)
    t, c, w = r // MR, r % MR // CAP, r % CAP
    m = np.zeros((QUAD, QUAD), np.float32)
    m[r, c * MR + t * CAP + w] = 1.0
    return m


def nt(a, b):
    return lax.dot_general(a, b, (((1,), (1,)), ((), ())), preferred_element_type=jnp.float32)


def nn(a, b):
    return jnp.dot(a, b, preferred_element_type=jnp.float32)


def step_dz(i):
    return 4 + (1 - 2 * (i % 2)) * ((i + 1) // 2)


def regroup_kernel(
    emb, ints, swap, out,
    slot_row, sent, got, own, other, hot, rank_col, rank_row, other_rank, best,
    send_sem, recv_sem, pair_send, pair_recv, rank_sem,
):
    blk, x = lax.axis_index("blk"), lax.axis_index("rep")
    z, y, core = blk // 8, (blk // 2) % 4, blk % 2
    me = blk * 4 + x

    def place(z2, d):
        y2 = (y + d // 8) % 4
        c2 = (core + d // 4 % 2) % 2
        x2 = (x + d % 4) % 4
        return z2 * PLANE + y2 * 8 + c2 * 4 + x2, (z2 * 8 + y2 * 2 + c2, x2)

    partner = (z * 8 + y * 2 + (1 - core), x)

    barrier = pltpu.get_barrier_semaphore()

    def greet(k, carry):
        _, device = place((z + k // PLANE) % 8, k % PLANE)
        pl.semaphore_signal(barrier, inc=1, device_id=device, device_id_type=MESH)
        return carry

    lax.fori_loop(1, DEV, greet, 0)

    a = lax.broadcasted_iota(jnp.int32, (256, 512), 0)
    b = lax.broadcasted_iota(jnp.int32, (256, 512), 1)
    prefix = jnp.where((a < b) | (b >= 256), 1.0, 0.0).astype(jnp.bfloat16)
    target_id = lax.broadcasted_iota(jnp.int32, (DEV, 256), 0)
    before = jnp.zeros((DEV, 256), jnp.float32)
    for i in range(ROWS // 256):
        target = ints[0:1, i * 256 : (i + 1) * 256] // ROWS
        one = jnp.where(target_id == target, 1.0, 0.0)
        counts = nn(one.astype(jnp.bfloat16), prefix)
        within = jnp.sum(one * (counts[:, :256] + before), axis=0, keepdims=True)
        before = before + counts[:, 256:]
        slot_row[0:1, i * 256 : (i + 1) * 256] = target * CAP + within.astype(jnp.int32)

    def pack(z2):
        def mark(h, carry):
            ids = lax.broadcasted_iota(jnp.int32, (48, ROWS), 0) + (z2 * GS + h * 48)
            hot[pl.ds(pl.multiple_of(h * 48, 48), 48), :] = jnp.where(
                ids == slot_row[0:1, :], 1.0, 0.0
            ).astype(jnp.bfloat16)
            return carry

        lax.fori_loop(0, GS // 48, mark, 0)
        for c in range(PARTS):
            part = nn(hot[...], emb[:, c * WIDE : (c + 1) * WIDE]).astype(jnp.bfloat16)
            own[0:GS, c * WIDE : (c + 1) * WIDE] = part

        def order(q, carry):
            rows = own[pl.ds(pl.multiple_of(q * 48, 48), 48), :]
            stack = jnp.concatenate([rows[:, c * WIDE : (c + 1) * WIDE] for c in range(PARTS)], axis=0)
            sent[pl.ds(pl.multiple_of(z2 * GR + q * QUAD, QUAD), QUAD), :] = nn(
                swap[...], stack
            ).astype(jnp.bfloat16)
            return carry

        lax.fori_loop(0, GS // 48, order, 0)

    def message(i, z2, d):
        to, device = place(z2, d)
        return pltpu.make_async_remote_copy(
            src_ref=sent.at[pl.ds(pl.multiple_of(to * MR, MR), MR)],
            dst_ref=got.at[pl.ds(pl.multiple_of(me * MR, MR), MR)],
            send_sem=send_sem.at[i],
            recv_sem=recv_sem.at[i],
            device_id=device,
            device_id_type=MESH,
        )

    def send(i, first):
        z2 = (z + step_dz(i)) % 8

        def one(d, carry):
            message(i, z2, d).start()
            return carry

        lax.fori_loop(first, PLANE, one, 0)

    pack((z + step_dz(0)) % 8)
    pl.semaphore_wait(barrier, DEV - 1)
    send(0, 0)

    def pack_and_send(i, carry):
        pack((z + step_dz(i)) % 8)
        send(i, 0)
        return carry

    lax.fori_loop(1, GROUPS - 1, pack_and_send, 0)
    pack(z)
    send(GROUPS - 1, 1)
    mine = pl.ds(pl.multiple_of(me * MR, MR), MR)
    pltpu.make_async_copy(sent.at[mine], got.at[mine], recv_sem.at[GROUPS - 1]).start()

    rank = ints[2:3, :] + 1
    pieces = jnp.concatenate(
        [
            (rank // 65536).astype(jnp.float32),
            (rank // 256 % 256).astype(jnp.float32),
            (rank % 256).astype(jnp.float32),
            jnp.zeros((5, ROWS), jnp.float32),
        ],
        axis=0,
    ).astype(jnp.bfloat16)

    def ranks(i, carry):
        z_src = (z - step_dz(i) + 8) % 8

        def mark(h, carry):
            ids = lax.broadcasted_iota(jnp.int32, (48, ROWS), 0) + (z_src * GS + h * 48)
            hot[pl.ds(pl.multiple_of(h * 48, 48), 48), :] = jnp.where(
                ids == ints[1:2, :], 1.0, 0.0
            ).astype(jnp.bfloat16)
            return carry

        lax.fori_loop(0, GS // 48, mark, 0)
        digits = nt(pieces, hot[...])
        value = digits[0:1] * 65536.0 + digits[1:2] * 256.0 + digits[2:3]
        value = jnp.where(value == 0.0, NOBODY, value)
        rank_row[i] = jnp.broadcast_to(value, (8, GS))
        rank_col[pl.ds(pl.multiple_of(i * GS, GS), GS), :] = jnp.broadcast_to(value, (128, GS)).T
        best[i] = jnp.full((8, GS), -1.0, jnp.float32)
        return carry

    lax.fori_loop(0, GROUPS, ranks, 0)
    rank_copy = pltpu.make_async_remote_copy(
        src_ref=rank_col, dst_ref=other_rank, send_sem=rank_sem.at[0], recv_sem=rank_sem.at[1],
        device_id=partner, device_id_type=MESH,
    )
    rank_copy.start()
    rank_copy.wait_recv()

    def group(i):
        return pl.ds(pl.multiple_of(i * GS, GS), GS)

    def block(rows, row_rank, i, j):
        score = nt(rows[group(i), :], own[group(j), :])
        earlier = row_rank[group(i), :]
        for c in range(GS // 128):
            lanes = slice(c * 128, (c + 1) * 128)
            kept = jnp.where(earlier < rank_row[j, 0:1, lanes], score[:, lanes], -1.0)
            top = jnp.max(kept, axis=0, keepdims=True)
            best[j, :, lanes] = jnp.maximum(best[j, :, lanes], jnp.broadcast_to(top, (8, 128)))

    def pair_copy(i):
        return pltpu.make_async_remote_copy(
            src_ref=own.at[group(i)], dst_ref=other.at[group(i)],
            send_sem=pair_send.at[i], recv_sem=pair_recv.at[i],
            device_id=partner, device_id_type=MESH,
        )

    def step(k, carry):
        z_src = (z - step_dz(k) + 8) % 8
        whole = pl.ds(pl.multiple_of(z_src * GR, GR), GR)
        pltpu.make_async_copy(got.at[whole], got.at[whole], recv_sem.at[k]).wait()

        def take(q, carry):
            rows = nn(swap[...], got[pl.ds(pl.multiple_of(z_src * GR + q * QUAD, QUAD), QUAD), :])
            cols = [rows[c * 48 : (c + 1) * 48, :] for c in range(PARTS)]
            square = cols[0] * cols[0]
            for c in range(1, PARTS):
                square = square + cols[c] * cols[c]
            mean = jnp.sum(square, axis=1, keepdims=True) * (1.0 / FEAT)
            scale = lax.rsqrt(mean + 1e-06) / math.sqrt(FEAT)
            place_rows = pl.ds(pl.multiple_of(k * GS + q * 48, 48), 48)
            for c in range(PARTS):
                own[place_rows, c * WIDE : (c + 1) * WIDE] = (cols[c] * scale).astype(jnp.bfloat16)
            return carry

        lax.fori_loop(0, GS // 48, take, 0)
        pair_copy(k).start()

        def first(j, carry):
            block(own, rank_col, j, k)
            block(other, other_rank, j, k)
            block(own, rank_col, k, j)
            return carry

        lax.fori_loop(0, k, first, 0)
        block(own, rank_col, k, k)
        pair_copy(k).wait_recv()

        def second(j, carry):
            block(other, other_rank, k, j)
            return carry

        lax.fori_loop(0, k + 1, second, 0)
        return carry

    lax.fori_loop(0, GROUPS, step, 0)

    def finish(i, carry):
        z_src = (z - step_dz(i) + 8) % 8
        for c in range(GS // 128):
            out[pl.ds(z_src * 3 + c, 1), :] = best[i, 0:1, c * 128 : (c + 1) * 128]
        pair_copy(i).wait_send()
        return carry

    lax.fori_loop(0, GROUPS, finish, 0)
    rank_copy.wait_send()

    def drain(i, carry):
        part = sent.at[pl.ds(pl.multiple_of(i * GR, GR), GR)]
        pltpu.make_async_copy(part, part, send_sem.at[i]).wait()
        return carry

    lax.fori_loop(0, GROUPS - 1, drain, 0)
    part = sent.at[pl.ds(0, GR - MR)]
    pltpu.make_async_copy(part, part, send_sem.at[GROUPS - 1]).wait()


def regroup(emb, ints, swap):
    vmem = pl.BlockSpec(memory_space=pltpu.VMEM)
    return pl.pallas_call(
        regroup_kernel,
        out_shape=jax.ShapeDtypeStruct((SLOTS // 128, 128), jnp.float32),
        in_specs=[vmem] * 3,
        out_specs=vmem,
        scratch_shapes=[
            pltpu.VMEM((8, ROWS), jnp.int32),
            pltpu.VMEM((DEV * MR, WIDE), jnp.bfloat16),
            pltpu.VMEM((DEV * MR, WIDE), jnp.bfloat16),
            pltpu.VMEM((SLOTS, FEAT), jnp.bfloat16),
            pltpu.VMEM((SLOTS, FEAT), jnp.bfloat16),
            pltpu.VMEM((GS, ROWS), jnp.bfloat16),
            pltpu.VMEM((SLOTS, 128), jnp.float32),
            pltpu.VMEM((GROUPS, 8, GS), jnp.float32),
            pltpu.VMEM((SLOTS, 128), jnp.float32),
            pltpu.VMEM((GROUPS, 8, GS), jnp.float32),
            pltpu.SemaphoreType.DMA((GROUPS,)),
            pltpu.SemaphoreType.DMA((GROUPS,)),
            pltpu.SemaphoreType.DMA((GROUPS,)),
            pltpu.SemaphoreType.DMA((GROUPS,)),
            pltpu.SemaphoreType.DMA((2,)),
        ],
        compiler_params=pltpu.CompilerParams(
            collective_id=0, has_side_effects=True, vmem_limit_bytes=58 * 2**20
        ),
    )(emb, ints, swap)


def pick_kernel(table, arrival, out):
    row, lane = arrival[...] // 128, arrival[...] % 128
    result = jnp.zeros(arrival.shape, jnp.float32)
    for r in range(SLOTS // 128):
        line = jnp.broadcast_to(table[r : r + 1, :], arrival.shape)
        result = jnp.where(row == r, jnp.take_along_axis(line, lane, axis=1), result)
    out[...] = result


def pick(table, arrival):
    return pl.pallas_call(
        pick_kernel, out_shape=jax.ShapeDtypeStruct((ROWS // 128, 128), jnp.float32)
    )(table, arrival.reshape(ROWS // 128, 128)).reshape(ROWS)


def on_device(embeddings, destination, arrival, dataset_index):
    block_id = lax.axis_index("blk") * lax.axis_size("rep") + lax.axis_index("rep")
    rank = lax.dynamic_slice_in_dim(dataset_index, block_id * ROWS, ROWS)
    ints = jnp.stack([destination, arrival, rank])
    table = regroup(embeddings, ints, jnp.asarray(swap_matrix(), jnp.bfloat16))
    return pick(table, arrival)


def solution(mesh):
    placed = (P(("blk", "rep"), None), P(("blk", "rep")), P(("blk", "rep")), P())
    return jax.shard_map(
        on_device, mesh=mesh, in_specs=placed, out_specs=P(("blk", "rep")), check_vma=False
    )
```

```python
import math

import jax
import jax.numpy as jnp
import numpy as np
from jax import lax
from jax.experimental import pallas as pl
from jax.experimental.pallas import tpu as pltpu
from jax.sharding import PartitionSpec as P

MESH = pl.DeviceIdType.MESH
ROWS = 2048
FEAT = 1024
CAP = 12
DEV = 256
PLANE = 32
GROUPS = 8
GS = PLANE * CAP
SLOTS = DEV * CAP
WIDE = 256
PARTS = FEAT // WIDE
MR = CAP * PARTS
QUAD = 4 * MR
GR = PLANE * MR
NOBODY = 2.0**23


def swap_matrix():
    r = np.arange(QUAD)
    t, c, w = r // MR, r % MR // CAP, r % CAP
    m = np.zeros((QUAD, QUAD), np.float32)
    m[r, c * MR + t * CAP + w] = 1.0
    return m


def nt(a, b):
    return lax.dot_general(a, b, (((1,), (1,)), ((), ())), preferred_element_type=jnp.float32)


def nn(a, b):
    return jnp.dot(a, b, preferred_element_type=jnp.float32)


def step_dz(i):
    return 4 + (1 - 2 * (i % 2)) * ((i + 1) // 2)


def regroup_kernel(
    emb, destination, arrival, dataset_index, swap, out,
    rows_in, rank_in, slot_row, sent, got, own, other, hot, rank_col, rank_row, other_rank, best, late,
    in_sem, send_sem, recv_sem, pair_send, pair_recv, rank_sem,
):
    blk, x = lax.axis_index("blk"), lax.axis_index("rep")
    z, y, core = blk // 8, (blk // 2) % 4, blk % 2
    me = blk * 4 + x
    partner = (z * 8 + y * 2 + (1 - core), x)

    def lane_pos(z2, y2, c2, x2):
        return (y2 * 2 + c2) * PLANE + z2 * 4 + x2

    load_rows = pltpu.make_async_copy(emb, rows_in, in_sem.at[0])
    load_rows.start()
    load_rank = pltpu.make_async_copy(
        dataset_index.at[:, pl.ds(pl.multiple_of(me * ROWS, ROWS), ROWS)], rank_in, in_sem.at[1]
    )
    load_rank.start()

    barrier = pltpu.get_barrier_semaphore()

    def greet(k, carry):
        z2, y2 = (z + k // 32) % 8, (y + k // 8) % 4
        c2, x2 = (core + k // 4 % 2) % 2, (x + k % 4) % 4
        pl.semaphore_signal(
            barrier, inc=1, device_id=(z2 * 8 + y2 * 2 + c2, x2), device_id_type=MESH
        )
        return carry

    lax.fori_loop(1, DEV, greet, 0)

    a = lax.broadcasted_iota(jnp.int32, (256, 512), 0)
    b = lax.broadcasted_iota(jnp.int32, (256, 512), 1)
    prefix = jnp.where((a < b) | (b >= 256), 1.0, 0.0).astype(jnp.bfloat16)
    target_id = lax.broadcasted_iota(jnp.int32, (DEV, 256), 0)
    before = jnp.zeros((DEV, 256), jnp.float32)
    for i in range(ROWS // 256):
        target = destination[0:1, i * 256 : (i + 1) * 256] // ROWS
        one = jnp.where(target_id == target, 1.0, 0.0)
        counts = nn(one.astype(jnp.bfloat16), prefix)
        within = jnp.sum(one * (counts[:, :256] + before), axis=0, keepdims=True)
        before = before + counts[:, 256:]
        slot_row[0:1, i * 256 : (i + 1) * 256] = target * CAP + within.astype(jnp.int32)

    def mark(ids_row, y2, c2):
        def one(h, carry):
            ids = lax.broadcasted_iota(jnp.int32, (48, ROWS), 0) + (h * GS + y2 * 96 + c2 * 48)
            hot[pl.ds(pl.multiple_of(h * 48, 48), 48), :] = jnp.where(
                ids == ids_row[0:1, :], 1.0, 0.0
            ).astype(jnp.bfloat16)
            return carry

        lax.fori_loop(0, GS // 48, one, 0)

    def pack(y2, c2):
        mark(slot_row, y2, c2)
        for c in range(PARTS):
            lanes = slice(c * WIDE, (c + 1) * WIDE)
            own[0:GS, lanes] = nn(hot[...], rows_in[:, lanes]).astype(jnp.bfloat16)
        base = (y2 * 2 + c2) * GR
        for q in range(GS // 48):
            stack = jnp.concatenate(
                [own[q * 48 : (q + 1) * 48, c * WIDE : (c + 1) * WIDE] for c in range(PARTS)], axis=0
            )
            sent[pl.ds(pl.multiple_of(base + q * QUAD, QUAD), QUAD), :] = nn(
                swap[...], stack
            ).astype(jnp.bfloat16)

    def message(i, y2, c2, d):
        z2, x2 = (z + step_dz(d % 8)) % 8, (x + 3 - d // 8) % 4
        return pltpu.make_async_remote_copy(
            src_ref=sent.at[pl.ds(pl.multiple_of(lane_pos(z2, y2, c2, x2) * MR, MR), MR)],
            dst_ref=got.at[pl.ds(pl.multiple_of(lane_pos(z, y, core, x) * MR, MR), MR)],
            send_sem=send_sem.at[i],
            recv_sem=recv_sem.at[i],
            device_id=(z2 * 8 + y2 * 2 + c2, x2),
            device_id_type=MESH,
        )

    def send(i, y2, c2, count):
        def one(d, carry):
            message(i, y2, c2, d).start()
            return carry

        lax.fori_loop(0, count, one, 0)

    load_rows.wait()
    pack(y, core)
    pl.semaphore_wait(barrier, DEV - 1)
    send(0, y, core, PLANE - 1)
    mine = pl.ds(pl.multiple_of(lane_pos(z, y, core, x) * MR, MR), MR)
    pltpu.make_async_copy(sent.at[mine], got.at[mine], recv_sem.at[0]).start()

    def pack_and_send(i, carry):
        y2, c2 = (y + i % 4) % 4, (core + i // 4) % 2
        pack(y2, c2)
        send(i, y2, c2, PLANE)
        return carry

    lax.fori_loop(1, GROUPS, pack_and_send, 0)

    load_rank.wait()
    rank = rank_in[...] + 1
    digits = jnp.concatenate(
        [
            jnp.broadcast_to(digit.astype(jnp.float32), (128, ROWS))
            for digit in (rank // 65536, rank // 256 % 256, rank % 256)
        ],
        axis=0,
    ).astype(jnp.bfloat16)

    def source(i):
        return (y + 4 - i % 4) % 4, (core + i // 4) % 2

    def group(i):
        return pl.ds(pl.multiple_of(i * GS, GS), GS)

    def ranks(i, carry):
        mark(arrival, *source(i))
        parts = nt(hot[...], digits)
        value = parts[:, :128] * 65536.0 + parts[:, 128:256] * 256.0 + parts[:, 256:]
        value = jnp.where(value == 0.0, NOBODY, value)
        rank_col[group(i), :] = value
        rank_row[i] = value.T[0:8]
        best[i] = jnp.full((8, GS), -1.0, jnp.float32)
        return carry

    lax.fori_loop(0, GROUPS, ranks, 0)
    rank_copy = pltpu.make_async_remote_copy(
        src_ref=rank_col, dst_ref=other_rank, send_sem=rank_sem.at[0], recv_sem=rank_sem.at[1],
        device_id=partner, device_id_type=MESH,
    )
    rank_copy.start()
    rank_copy.wait_recv()

    def fold(kept):
        return jnp.max(kept.reshape(GS // 8, 8, 128), axis=0)

    def block(rows, row_rank, i, j):
        score = nt(rows[group(i), :], own[group(j), :])
        for c in range(GS // 128):
            lanes = slice(c * 128, (c + 1) * 128)
            earlier = row_rank[group(i), :] < rank_row[j, 0:1, lanes]
            kept = jnp.where(earlier, score[:, lanes], -1.0)
            best[j, :, lanes] = jnp.maximum(best[j, :, lanes], fold(kept))

    def both(i, j):
        score = nt(own[group(i), :], own[group(j), :])
        for c in range(GS // 128):
            lanes = slice(c * 128, (c + 1) * 128)
            earlier = rank_col[group(i), :] < rank_row[j, 0:1, lanes]
            kept = jnp.where(earlier, score[:, lanes], -1.0)
            best[j, :, lanes] = jnp.maximum(best[j, :, lanes], fold(kept))
            late[...] = jnp.maximum(late[...], jnp.where(earlier, -1.0, score[:, lanes]))

    def pair_copy(i):
        return pltpu.make_async_remote_copy(
            src_ref=own.at[group(i)], dst_ref=other.at[group(i)],
            send_sem=pair_send.at[i], recv_sem=pair_recv.at[i],
            device_id=partner, device_id_type=MESH,
        )

    def step(k, carry):
        y2, c2 = source(k)
        base = (y2 * 2 + c2) * GR
        whole = pl.ds(pl.multiple_of(base, GR), GR)
        pltpu.make_async_copy(got.at[whole], got.at[whole], recv_sem.at[k]).wait()
        for q in range(GS // 48):
            rows = nn(swap[...], got[pl.ds(pl.multiple_of(base + q * QUAD, QUAD), QUAD), :])
            cols = [rows[c * 48 : (c + 1) * 48, :] for c in range(PARTS)]
            square = cols[0] * cols[0]
            for c in range(1, PARTS):
                square = square + cols[c] * cols[c]
            mean = jnp.sum(square, axis=1, keepdims=True) * (1.0 / FEAT)
            scale = lax.rsqrt(mean + 1e-06) / math.sqrt(FEAT)
            place_rows = pl.ds(pl.multiple_of(k * GS + q * 48, 48), 48)
            for c in range(PARTS):
                own[place_rows, c * WIDE : (c + 1) * WIDE] = (cols[c] * scale).astype(jnp.bfloat16)
        pair_copy(k).start()
        late[...] = jnp.full((GS, 128), -1.0, jnp.float32)

        def first(j, carry):
            both(k, j)
            block(other, other_rank, j, k)
            return carry

        lax.fori_loop(0, k, first, 0)
        block(own, rank_col, k, k)
        best[k] = jnp.maximum(best[k], jnp.max(late[...].T, axis=0, keepdims=True))
        pair_copy(k).wait_recv()

        def second(j, carry):
            block(other, other_rank, k, j)
            return carry

        lax.fori_loop(0, k + 1, second, 0)
        return carry

    lax.fori_loop(0, GROUPS, step, 0)

    def finish(i, carry):
        y2, c2 = source(i)
        top = jnp.max(best[i], axis=0, keepdims=True)
        for c in range(GS // 128):
            out[pl.ds((y2 * 2 + c2) * 3 + c, 1), :] = top[:, c * 128 : (c + 1) * 128]
        pair_copy(i).wait_send()
        return carry

    lax.fori_loop(0, GROUPS, finish, 0)
    rank_copy.wait_send()

    part = sent.at[pl.ds(0, GR - MR)]
    pltpu.make_async_copy(part, part, send_sem.at[0]).wait()

    def drain(i, carry):
        part = sent.at[pl.ds(pl.multiple_of(i * GR, GR), GR)]
        pltpu.make_async_copy(part, part, send_sem.at[i]).wait()
        return carry

    lax.fori_loop(1, GROUPS, drain, 0)


def regroup(emb, destination, arrival, dataset_index, swap):
    vmem, anywhere = pl.BlockSpec(memory_space=pltpu.VMEM), pl.BlockSpec(memory_space=pl.ANY)
    return pl.pallas_call(
        regroup_kernel,
        out_shape=jax.ShapeDtypeStruct((SLOTS // 128, 128), jnp.float32),
        in_specs=[anywhere, vmem, vmem, anywhere, vmem],
        out_specs=vmem,
        scratch_shapes=[
            pltpu.VMEM((ROWS, FEAT), jnp.bfloat16),
            pltpu.VMEM((1, ROWS), jnp.int32),
            pltpu.VMEM((1, ROWS), jnp.int32),
            pltpu.VMEM((DEV * MR, WIDE), jnp.bfloat16),
            pltpu.VMEM((DEV * MR, WIDE), jnp.bfloat16),
            pltpu.VMEM((SLOTS, FEAT), jnp.bfloat16),
            pltpu.VMEM((SLOTS, FEAT), jnp.bfloat16),
            pltpu.VMEM((GS, ROWS), jnp.bfloat16),
            pltpu.VMEM((SLOTS, 128), jnp.float32),
            pltpu.VMEM((GROUPS, 8, GS), jnp.float32),
            pltpu.VMEM((SLOTS, 128), jnp.float32),
            pltpu.VMEM((GROUPS, 8, GS), jnp.float32),
            pltpu.VMEM((GS, 128), jnp.float32),
            pltpu.SemaphoreType.DMA((2,)),
            pltpu.SemaphoreType.DMA((GROUPS,)),
            pltpu.SemaphoreType.DMA((GROUPS,)),
            pltpu.SemaphoreType.DMA((GROUPS,)),
            pltpu.SemaphoreType.DMA((GROUPS,)),
            pltpu.SemaphoreType.DMA((2,)),
        ],
        compiler_params=pltpu.CompilerParams(
            collective_id=0, has_side_effects=True, vmem_limit_bytes=58 * 2**20
        ),
    )(emb, destination, arrival, dataset_index, swap)


def pick_kernel(table, arrival, out):
    source, rest = arrival[...] // 48, arrival[...] % 48
    column = source // 8 * 48 + rest
    row, lane = source % 8 * 3 + column // 128, column % 128
    result = jnp.zeros(arrival.shape, jnp.float32)
    for r in range(SLOTS // 128):
        line = jnp.broadcast_to(table[r : r + 1, :], arrival.shape)
        result = jnp.where(row == r, jnp.take_along_axis(line, lane, axis=1), result)
    out[...] = result


def pick(table, arrival):
    return pl.pallas_call(
        pick_kernel, out_shape=jax.ShapeDtypeStruct((ROWS // 128, 128), jnp.float32)
    )(table, arrival.reshape(ROWS // 128, 128)).reshape(ROWS)


def on_device(embeddings, destination, arrival, dataset_index):
    table = regroup(
        embeddings,
        destination.reshape(1, ROWS),
        arrival.reshape(1, ROWS),
        dataset_index.reshape(1, -1),
        jnp.asarray(swap_matrix(), jnp.bfloat16),
    )
    return pick(table, arrival)


def solution(mesh):
    placed = (P(("blk", "rep"), None), P(("blk", "rep")), P(("blk", "rep")), P())
    return jax.shard_map(
        on_device, mesh=mesh, in_specs=placed, out_specs=P(("blk", "rep")), check_vma=False
    )
```

```python
import math

import jax
import jax.numpy as jnp
import numpy as np
from jax import lax
from jax.experimental import pallas as pl
from jax.experimental.pallas import tpu as pltpu
from jax.sharding import PartitionSpec as P

MESH = pl.DeviceIdType.MESH
ROWS = 2048
FEAT = 1024
CAP = 12
DEV = 256
PLANE = 32
GROUPS = 8
GS = PLANE * CAP
SLOTS = DEV * CAP
WIDE = 256
PARTS = FEAT // WIDE
MR = CAP * PARTS
QUAD = 4 * MR
GR = PLANE * MR
LAST = GROUPS - 1
ORDER = (4, 2, 6, 0, 3, 5, 1, 7)
EARLY = 4
PART = (EARLY * 48, (8 - EARLY) * 48)
LANE = (LAST * GS, (LAST + 1) * GS)
LANES = LANE[1] + 256
CHUNK = 512
NOBODY = 2.0**23


def swap_matrix():
    r = np.arange(QUAD)
    t, c, w = r // MR, r % MR // CAP, r % CAP
    m = np.zeros((QUAD, QUAD), np.float32)
    m[r, c * MR + t * CAP + w] = 1.0
    return m


def nt(a, b):
    return lax.dot_general(a, b, (((1,), (1,)), ((), ())), preferred_element_type=jnp.float32)


def nn(a, b):
    return jnp.dot(a, b, preferred_element_type=jnp.float32)


def regroup_kernel(
    emb, destination, arrival, dataset_index, swap, out,
    rows_in, rank_in, slot_row, sent, got, own, other, hot, rank_col, rank_row, other_rank, best, late,
    in_sem, send_sem, recv_sem, pair_send, pair_recv, rank_sem, ready,
):
    blk, x = lax.axis_index("blk"), lax.axis_index("rep")
    z, y, core = blk // 8, (blk // 2) % 4, blk % 2
    me = blk * 4 + x
    partner = (z * 8 + y * 2 + (1 - core), x)

    def lane_pos(z2, y2, c2, x2):
        return (y2 * 2 + c2) * PLANE + z2 * 4 + x2

    load_rows = pltpu.make_async_copy(emb, rows_in, in_sem.at[0])
    load_rows.start()
    load_rank = pltpu.make_async_copy(
        dataset_index.at[:, pl.ds(pl.multiple_of(me * ROWS, ROWS), ROWS)], rank_in, in_sem.at[1]
    )
    load_rank.start()

    barrier = pltpu.get_barrier_semaphore()

    def in_layer(k):
        return lax.rem(z + k // 4, 8) * 8 + y * 2 + core, lax.rem(x + k % 4, 4)

    def in_column(k):
        return z * 8 + lax.rem(y + k // 2, 4) * 2 + lax.rem(core + k % 2, 2), x

    def greet_layer(k, carry):
        pl.semaphore_signal(barrier, inc=1, device_id=in_layer(k), device_id_type=MESH)
        return carry

    def greet_column(k, carry):
        pl.semaphore_signal(barrier, inc=1, device_id=in_column(k), device_id_type=MESH)
        return carry

    lax.fori_loop(1, 32, greet_layer, 0)
    lax.fori_loop(1, 8, greet_column, 0)

    a = lax.broadcasted_iota(jnp.int32, (256, 512), 0)
    b = lax.broadcasted_iota(jnp.int32, (256, 512), 1)
    prefix = jnp.where((a < b) | (b >= 256), 1.0, 0.0).astype(jnp.bfloat16)
    target_id = lax.broadcasted_iota(jnp.int32, (DEV, 256), 0)
    before = jnp.zeros((DEV, 256), jnp.float32)
    for i in range(ROWS // 256):
        target = destination[0:1, i * 256 : (i + 1) * 256] // ROWS
        one = jnp.where(target_id == target, 1.0, 0.0)
        counts = nn(one.astype(jnp.bfloat16), prefix)
        within = jnp.sum(one * (counts[:, :256] + before), axis=0, keepdims=True)
        before = before + counts[:, 256:]
        slot_row[0:1, i * 256 : (i + 1) * 256] = target * CAP + within.astype(jnp.int32)

    def mark_one(ids_row, y2, c2, h, z2):
        ids = lax.broadcasted_iota(jnp.int32, (48, ROWS), 0) + (z2 * GS + y2 * 96 + c2 * 48)
        hot[pl.ds(pl.multiple_of(h * 48, 48), 48), :] = jnp.where(
            ids == ids_row[0:1, :], 1.0, 0.0
        ).astype(jnp.bfloat16)

    def mark(ids_row, y2, c2):
        def one(h, carry):
            mark_one(ids_row, y2, c2, h, h)
            return carry

        lax.fori_loop(0, GS // 48, one, 0)

    def pack(y2, c2):
        mark(slot_row, y2, c2)
        for c in range(PARTS):
            lanes = slice(c * WIDE, (c + 1) * WIDE)
            own[0:GS, lanes] = nn(hot[...], rows_in[:, lanes]).astype(jnp.bfloat16)
        base = (y2 * 2 + c2) * GR
        for q in range(GS // 48):
            stack = jnp.concatenate(
                [own[q * 48 : (q + 1) * 48, c * WIDE : (c + 1) * WIDE] for c in range(PARTS)], axis=0
            )
            sent[pl.ds(pl.multiple_of(base + q * QUAD, QUAD), QUAD), :] = nn(
                swap[...], stack
            ).astype(jnp.bfloat16)

    def message(i, y2, c2, dz, dx):
        z2, x2 = lax.rem(z + dz, 8), lax.rem(x + dx, 4)
        late_part = 1 if dz in ORDER[EARLY:] else 0
        return pltpu.make_async_remote_copy(
            src_ref=sent.at[pl.ds(pl.multiple_of(lane_pos(z2, y2, c2, x2) * MR, MR), MR)],
            dst_ref=got.at[pl.ds(pl.multiple_of(lane_pos(z, y, core, x) * MR, MR), MR)],
            send_sem=send_sem.at[i],
            recv_sem=recv_sem.at[i + i // LAST * late_part],
            device_id=(z2 * 8 + y2 * 2 + c2, x2),
            device_id_type=MESH,
        )

    def send(i, y2, c2, own_layer):
        for dz in ORDER:

            def one(dx, carry, dz=dz):
                message(i, y2, c2, dz, dx).start()
                return carry

            lax.fori_loop(1 if own_layer and dz == 0 else 0, 4, one, 0)

    load_rows.wait()
    pack(y, core)
    pl.semaphore_wait(barrier, 38)
    send(0, y, core, True)

    def tell(k, carry):
        pl.semaphore_signal(ready, inc=1, device_id=in_column(k), device_id_type=MESH)
        return carry

    lax.fori_loop(1, 8, tell, 0)
    mine = pl.ds(pl.multiple_of(lane_pos(z, y, core, x) * MR, MR), MR)
    pltpu.make_async_copy(sent.at[mine], got.at[mine], recv_sem.at[0]).start()
    pl.semaphore_wait(ready, 7)

    def pack_and_send(i, carry):
        y2, c2 = (y + i % 4) % 4, (core + i // 4) % 2
        pack(y2, c2)
        send(i, y2, c2, False)
        return carry

    lax.fori_loop(1, GROUPS, pack_and_send, 0)

    load_rank.wait()
    rank = rank_in[...] + 1
    digits = jnp.concatenate(
        [
            jnp.broadcast_to(digit.astype(jnp.float32), (128, ROWS))
            for digit in (rank // 65536, rank // 256 % 256, rank % 256)
        ],
        axis=0,
    ).astype(jnp.bfloat16)

    def source(i):
        return (y + 4 - i % 4) % 4, (core + i // 4) % 2

    def group(i):
        return pl.ds(pl.multiple_of(i * GS, GS), GS)

    def known(value):
        return jnp.where(value == 0.0, NOBODY, value)

    def columns(rows):
        parts = nt(rows, digits)
        return known(parts[:, :128] * 65536.0 + parts[:, 128:256] * 256.0 + parts[:, 256:])

    def lanes_of(rows):
        parts = [nt(digits[c * 128 : c * 128 + 16], rows) for c in range(3)]
        return known(parts[0] * 65536.0 + parts[1] * 256.0 + parts[2])[0:8]

    def ranks(i, carry):
        mark(arrival, *source(i))
        value = columns(hot[...])
        rank_col[group(i), :] = value
        rank_row[:, group(i)] = value.T[0:8]
        return carry

    lax.fori_loop(0, LAST, ranks, 0)
    for h, dz in enumerate(ORDER):
        mark_one(arrival, *source(LAST), h, lax.rem(z + 8 - dz, 8))
    rank_col[group(LAST), :] = columns(hot[...])
    for s in range(2):
        first_row = s * PART[0]
        rank_row[:, LANE[s] : LANE[s] + PART[s]] = lanes_of(
            hot[first_row : first_row + PART[s], :]
        )
    best[...] = jnp.full((8, LANES), -1.0, jnp.float32)
    rank_copy = pltpu.make_async_remote_copy(
        src_ref=rank_col, dst_ref=other_rank, send_sem=rank_sem.at[0], recv_sem=rank_sem.at[1],
        device_id=partner, device_id_type=MESH,
    )
    rank_copy.start()
    rank_copy.wait_recv()

    def block(rows, row_rank, at, cols, lane, follow=False):
        score = nt(rows[at, :], own[cols, :])
        count, width = score.shape
        for lo in range(0, width, 128):
            w = min(128, width - lo)
            lanes = pl.ds(lane + lo if isinstance(lane, int) else pl.multiple_of(lane + lo, 128), w)
            mine = score[:, lo : lo + w]
            earlier = row_rank[at, :w] < rank_row[0:1, lanes]
            kept = jnp.where(earlier, mine, -1.0)
            top = jnp.max(kept.reshape(count // 8, 8, w), axis=0)
            best[:, lanes] = jnp.maximum(best[:, lanes], top)
            if follow:
                late[:count, :w] = jnp.maximum(late[:count, :w], jnp.where(earlier, -1.0, mine))

    def pair_copy(k, at):
        return pltpu.make_async_remote_copy(
            src_ref=own.at[at], dst_ref=other.at[at],
            send_sem=pair_send.at[k], recv_sem=pair_recv.at[k],
            device_id=partner, device_id_type=MESH,
        )

    def take(row, at):
        rows = nn(swap[...], got[pl.ds(pl.multiple_of(row, QUAD), QUAD), :])
        cols = [rows[c * 48 : (c + 1) * 48, :] for c in range(PARTS)]
        square = cols[0] * cols[0]
        for c in range(1, PARTS):
            square = square + cols[c] * cols[c]
        mean = jnp.sum(square, axis=1, keepdims=True) * (1.0 / FEAT)
        scale = lax.rsqrt(mean + 1e-06) / math.sqrt(FEAT)
        for c in range(PARTS):
            own[pl.ds(pl.multiple_of(at, 48), 48), c * WIDE : (c + 1) * WIDE] = (
                cols[c] * scale
            ).astype(jnp.bfloat16)

    def settle(lane, width):
        lanes = pl.ds(lane, width)
        top = jnp.max(late[...].T, axis=0, keepdims=True)
        best[:, lanes] = jnp.maximum(best[:, lanes], top[:, :width])

    def step(k, carry):
        y2, c2 = source(k)
        base = (y2 * 2 + c2) * GR
        whole = got.at[pl.ds(pl.multiple_of(base, GR), GR)]
        pltpu.make_async_copy(whole, whole, recv_sem.at[k]).wait()
        for q in range(GS // 48):
            take(base + q * QUAD, k * GS + q * 48)
        pair_copy(k, group(k)).start()
        late[...] = jnp.full((GS, 128), -1.0, jnp.float32)

        def first(j, carry):
            block(own, rank_col, group(k), group(j), j * GS, follow=True)
            block(other, other_rank, group(j), group(k), k * GS)
            return carry

        lax.fori_loop(0, k, first, 0)
        block(own, rank_col, group(k), group(k), k * GS)
        settle(pl.multiple_of(k * GS, GS), GS)
        pair_copy(k, group(k)).wait_recv()

        def second(j, carry):
            block(other, other_rank, group(k), group(j), j * GS)
            return carry

        lax.fori_loop(0, k + 1, second, 0)
        return carry

    lax.fori_loop(0, LAST, step, 0)

    parts = [pl.ds(LAST * GS + s * PART[0], PART[s]) for s in range(2)]

    def against_own(rows, row_rank, at, follow):
        def some(j, carry):
            block(rows, row_rank, at, pl.ds(pl.multiple_of(j * CHUNK, CHUNK), CHUNK), j * CHUNK, follow)
            return carry

        whole = LANE[0] // CHUNK
        lax.fori_loop(0, whole, some, 0)
        rest = LANE[0] - whole * CHUNK
        block(rows, row_rank, at, pl.ds(whole * CHUNK, rest), whole * CHUNK, follow)

    y2, c2 = source(LAST)
    base = (y2 * 2 + c2) * GR
    for s in range(2):
        at, k = parts[s], LAST + s
        part = got.at[pl.ds(0, PART[s] * PARTS)]
        pltpu.make_async_copy(part, part, recv_sem.at[k]).wait()
        for q in range(PART[s] // 48):
            z_src = lax.rem(z + 8 - ORDER[s * EARLY + q], 8)
            take(base + z_src * QUAD, LAST * GS + s * PART[0] + q * 48)
        pair_copy(k, at).start()
        late[...] = jnp.full((GS, 128), -1.0, jnp.float32)
        against_own(own, rank_col, at, True)

        def from_other(j, carry):
            block(other, other_rank, group(j), at, LANE[s])
            return carry

        lax.fori_loop(0, LAST, from_other, 0)
        if s == 1:
            block(own, rank_col, at, parts[0], LANE[0], follow=True)
        block(own, rank_col, at, at, LANE[s])
        settle(LANE[s], PART[s])

    for s in range(2):
        pair_copy(LAST + s, parts[s]).wait_recv()
    against_own(other, other_rank, group(LAST), False)
    for s in range(2):
        block(other, other_rank, group(LAST), parts[s], LANE[s])

    top = jnp.max(best[...], axis=0, keepdims=True)
    for r in range(LANES // 128):
        out[r : r + 1, :] = top[:, r * 128 : (r + 1) * 128]

    def close(i, carry):
        pair_copy(i, group(i)).wait_send()
        return carry

    lax.fori_loop(0, LAST, close, 0)
    for s in range(2):
        pair_copy(LAST + s, parts[s]).wait_send()
    rank_copy.wait_send()

    part = sent.at[pl.ds(0, GR - MR)]
    pltpu.make_async_copy(part, part, send_sem.at[0]).wait()

    def drain(i, carry):
        part = sent.at[pl.ds(pl.multiple_of(i * GR, GR), GR)]
        pltpu.make_async_copy(part, part, send_sem.at[i]).wait()
        return carry

    lax.fori_loop(1, GROUPS, drain, 0)


def regroup(emb, destination, arrival, dataset_index, swap):
    vmem, anywhere = pl.BlockSpec(memory_space=pltpu.VMEM), pl.BlockSpec(memory_space=pl.ANY)
    return pl.pallas_call(
        regroup_kernel,
        out_shape=jax.ShapeDtypeStruct((LANES // 128, 128), jnp.float32),
        in_specs=[anywhere, vmem, vmem, anywhere, vmem],
        out_specs=vmem,
        scratch_shapes=[
            pltpu.VMEM((ROWS, FEAT), jnp.bfloat16),
            pltpu.VMEM((1, ROWS), jnp.int32),
            pltpu.VMEM((1, ROWS), jnp.int32),
            pltpu.VMEM((DEV * MR, WIDE), jnp.bfloat16),
            pltpu.VMEM((DEV * MR, WIDE), jnp.bfloat16),
            pltpu.VMEM((SLOTS, FEAT), jnp.bfloat16),
            pltpu.VMEM((SLOTS, FEAT), jnp.bfloat16),
            pltpu.VMEM((GS, ROWS), jnp.bfloat16),
            pltpu.VMEM((SLOTS, 128), jnp.float32),
            pltpu.VMEM((8, LANES), jnp.float32),
            pltpu.VMEM((SLOTS, 128), jnp.float32),
            pltpu.VMEM((8, LANES), jnp.float32),
            pltpu.VMEM((GS, 128), jnp.float32),
            pltpu.SemaphoreType.DMA((2,)),
            pltpu.SemaphoreType.DMA((GROUPS,)),
            pltpu.SemaphoreType.DMA((GROUPS + 1,)),
            pltpu.SemaphoreType.DMA((GROUPS + 1,)),
            pltpu.SemaphoreType.DMA((GROUPS + 1,)),
            pltpu.SemaphoreType.DMA((2,)),
            pltpu.SemaphoreType.REGULAR,
        ],
        compiler_params=pltpu.CompilerParams(
            collective_id=0, has_side_effects=True, vmem_limit_bytes=58 * 2**20
        ),
    )(emb, destination, arrival, dataset_index, swap)


def pick_kernel(table, arrival, out):
    blk = lax.axis_index("blk")
    z, y, core = blk // 8, (blk // 2) % 4, blk % 2
    source, rest = arrival[...] // 48, arrival[...] % 48
    z_src, y_src, c_src = source // 8, source // 2 % 4, source % 2
    step = (y - y_src + 4) % 4 + (c_src - core + 2) % 2 * 4
    lane = step * GS + z_src * 48
    offset = (z - z_src + 8) % 8
    for q, dz in enumerate(ORDER):
        at = LANE[0] + q * 48 if q < EARLY else LANE[1] + (q - EARLY) * 48
        lane = jnp.where((step == LAST) & (offset == dz), at, lane)
    lane = lane + rest
    row, lane = lane // 128, lane % 128
    result = jnp.zeros(arrival.shape, jnp.float32)
    for r in range(LANES // 128):
        line = jnp.broadcast_to(table[r : r + 1, :], arrival.shape)
        result = jnp.where(row == r, jnp.take_along_axis(line, lane, axis=1), result)
    out[...] = result


def pick(table, arrival):
    return pl.pallas_call(
        pick_kernel, out_shape=jax.ShapeDtypeStruct((ROWS // 128, 128), jnp.float32)
    )(table, arrival.reshape(ROWS // 128, 128)).reshape(ROWS)


def on_device(embeddings, destination, arrival, dataset_index):
    table = regroup(
        embeddings,
        destination.reshape(1, ROWS),
        arrival.reshape(1, ROWS),
        dataset_index.reshape(1, -1),
        jnp.asarray(swap_matrix(), jnp.bfloat16),
    )
    return pick(table, arrival)


def solution(mesh):
    placed = (P(("blk", "rep"), None), P(("blk", "rep")), P(("blk", "rep")), P())
    return jax.shard_map(
        on_device, mesh=mesh, in_specs=placed, out_specs=P(("blk", "rep")), check_vma=False
    )
```
